32 devices in a mesh: band: 8 (over y, x, core), lev: 4 (over z).
Axes of the slice: x: 2, y: 2, z: 4, core: 2. Of those that a mesh axis runs over, the one named last changes fastest.
Arguments:
- columns: bfloat16 [128, 48, 192, 128], P('band', 'lev'), may hold values from -6 to 6
- vertical: bfloat16 [64, 64], replicated
- row_len: int32 [128], P('band'), may hold values from 20 to 5136, as said below
- wave_order: int32 [1280], replicated, may hold values from 0 to 1279, each once
- legendre: bfloat16 [1280, 128, 1280], P('band'), may hold values from -0.5 to 0.5
Outputs:
- spectra: bfloat16 [1280, 2, 192, 1280], P('band', None, 'lev')
The draws below stay inside these ranges and needn't reach their ends.
Inputs may be any that keep to these rules, and one draw needn't show every extreme that they name: `row_len`: row lengths are 4 i + 16 for latitude indices i that rise strictly from row to row; the last row is the longest. `wave_order`: each wavenumber appears once.
All inputs are finite; a program needn't handle non-finite values.
Results may differ from the reference program's by a relative error of at most 0.0062.
Values may be sent and summed in bfloat16 or wider, within the bound.
A program may use at most 320 MiB of HBM per device.

```python
import jax
import jax.numpy as jnp
from jax import lax

OCT_LATS = 1280
MW = 1280
LEVELS = 64
ROWBLK = 48
NLAT = 128
CHANNELS = 192


def draw_row_len(key, part):
    key = jax.random.fold_in(key, 5)
    shuffled = jax.random.permutation(key, OCT_LATS - 1).astype(jnp.int32)
    chosen = jnp.sort(shuffled[:NLAT - 1]) + 1
    latitude = jnp.concatenate([chosen, jnp.full((1,), OCT_LATS, jnp.int32)])
    return (4 * latitude + 16).astype(jnp.int32)


def draw_vertical(key, part):
    key = jax.random.fold_in(key, 7)
    positions = jnp.arange(LEVELS)
    distance = jnp.abs(positions[:, None] - positions[None, :])
    spread = jax.random.uniform(key, (LEVELS, LEVELS), jnp.float32, -0.35, 0.35)
    banded = jnp.where((distance <= 4) & (distance > 0), spread, 0.0)
    return (jnp.eye(LEVELS, dtype=jnp.float32) + banded).astype(jnp.bfloat16)


def shard_levels(stream_key, shape, pieces, low, largest):
    loudness = 1.0
    for axis_at, blocks in pieces:
        heights = jax.random.uniform(jax.random.fold_in(jax.random.fold_in(stream_key, 6), axis_at), (blocks,), jnp.float32, low / len(pieces), largest / len(pieces))
        loudness = loudness * jnp.repeat(jnp.exp(heights), shape[axis_at] // blocks).reshape((-1,) + (1,) * (len(shape) - 1 - axis_at))
    return loudness


def gaussian(key, dims, scale, bound, pieces=(), kind=jnp.bfloat16):
    gain = shard_levels(key, dims, pieces, -0.22, 0.18) if pieces else 1.0
    drawn = jax.random.normal(key, dims, jnp.float32) * scale * gain
    return jnp.minimum(jnp.maximum(drawn, -bound), bound).astype(kind)


def setup_inputs(seed: int = 0) -> dict:
    streams_of = jax.random.split(jax.random.key(seed), 6)
    columns = gaussian(streams_of[0], (NLAT, ROWBLK, CHANNELS, 128), 1.0, 6.0, ((0, 8), (1, 4)))
    vertical = draw_vertical(jax.random.fold_in(streams_of[5], 71), 0)
    row_len = draw_row_len(jax.random.fold_in(streams_of[5], 71), 0)
    wave_order = jax.random.permutation(streams_of[3], MW).astype(jnp.int32)
    legendre = gaussian(streams_of[4], (MW, NLAT, MW), NLAT ** -0.5, 0.5, ((0, 8),))
    return {"columns": columns, "vertical": vertical, "row_len": row_len, "wave_order": wave_order, "legendre": legendre}


def fourier_table(wave_list, length, first_point, points):
    block_count = points // 128
    block_start = first_point + 128 * jnp.arange(block_count, dtype=jnp.int32)
    inner = jnp.arange(128, dtype=jnp.int32)
    step_angle = 6.283185307179586 / length.astype(jnp.float32)
    outer_angle = (block_start[:, None] * wave_list[None, :] % length).astype(jnp.float32) * step_angle
    inner_angle = (inner[:, None] * wave_list[None, :] % length).astype(jnp.float32) * step_angle
    outer_cos = jnp.cos(outer_angle)[:, None, :]
    outer_sin = jnp.sin(outer_angle)[:, None, :]
    inner_cos = jnp.cos(inner_angle)[None, :, :]
    inner_sin = jnp.sin(inner_angle)[None, :, :]
    cosine = (outer_cos * inner_cos - outer_sin * inner_sin).reshape(points, -1)
    minus_sine = (-(outer_sin * inner_cos + outer_cos * inner_sin)).reshape(points, -1)
    positions = first_point + jnp.arange(points, dtype=jnp.int32)
    inside = (positions < length)[:, None]
    cosine = jnp.where(inside, cosine, 0.0)
    minus_sine = jnp.where(inside, minus_sine, 0.0)
    return jnp.stack([cosine, minus_sine], axis=1).astype(jnp.bfloat16)

def reference(columns, vertical, row_len, wave_order, legendre):
    row_count, block_count, channels, block_width = columns.shape
    levels = vertical.shape[0]
    wave_count = wave_order.shape[0]

    def one_row(row_item):
        row_block, length = row_item
        shaped = row_block.reshape(block_count, channels // levels, levels, block_width).astype(jnp.float32)
        lifted = jnp.einsum('ml,bflp->bfmp', vertical.astype(jnp.float32), shaped).astype(jnp.bfloat16)
        lifted = lifted.reshape(block_count, channels, block_width)
        fourier = fourier_table(wave_order, length, 0, block_count * block_width)
        fourier = fourier.reshape(block_count, block_width, 2, wave_count)
        summed = jnp.einsum('bcp,bpqs->cqs', lifted.astype(jnp.float32), fourier.astype(jnp.float32))
        return (summed * lax.rsqrt(length.astype(jnp.float32))).astype(jnp.bfloat16)
    coeffs = lax.map(one_row, (columns, row_len))
    by_slot = jnp.moveaxis(coeffs, 3, 0)

    def one_slot(row_item):
        slot_coeffs, slot_table, wave_number = row_item
        accumulated = jnp.einsum('rcq,rn->qcn', slot_coeffs.astype(jnp.float32), slot_table.astype(jnp.float32))
        upper_part = jnp.arange(wave_count, dtype=jnp.int32) >= wave_number
        return jnp.where(upper_part[None, None, :], accumulated, 0.0).astype(jnp.bfloat16)
    return lax.map(one_slot, (by_slot, legendre, wave_order))
```

```python
import functools
import math

import jax
import jax.numpy as jnp
from jax import lax
from jax.experimental import pallas as pl
from jax.experimental.pallas import tpu as pltpu
from jax.sharding import PartitionSpec as P

CHUNKS = 2
LONGEST = 5136
FINE = 16
COARSE = 32
SPAN = FINE * COARSE
TILE = 256
SLOTS = 4


def lift_kernel(scal_ref, w_ref, x_ref, o_ref, *, row_at, rows):
    length = scal_ref[row_at + pl.program_id(0)]
    first = scal_ref[rows]
    targets, _, blocks, share, width = o_ref.shape
    for b in range(0, blocks, 2):
        pair = jnp.concatenate([x_ref[0, b], x_ref[0, b + 1]], axis=1)
        y = jnp.dot(w_ref[...], pair, preferred_element_type=jnp.float32)
        spot = first + b * width + lax.broadcasted_iota(jnp.int32, y.shape, 1)
        y = jnp.where(spot < length, y, 0.0)
        for h in range(2):
            part = y[:, h * width : (h + 1) * width].reshape(targets, share, width)
            o_ref[:, 0, b + h] = part.astype(jnp.bfloat16)


def lift(columns, weight, scal, row_at, rows_part, targets):
    rows, blocks, channels, width = columns.shape
    share = channels // targets
    return pl.pallas_call(
        functools.partial(lift_kernel, row_at=row_at, rows=rows),
        grid_spec=pltpu.PrefetchScalarGridSpec(
            num_scalar_prefetch=1,
            grid=(rows_part,),
            in_specs=[
                pl.BlockSpec((channels, channels), lambda i, s: (0, 0)),
                pl.BlockSpec((1, blocks, channels, width), lambda i, s: (row_at + i, 0, 0, 0)),
            ],
            out_specs=pl.BlockSpec((targets, 1, blocks, share, width), lambda i, s: (0, i, 0, 0, 0)),
        ),
        out_shape=jax.ShapeDtypeStruct((targets, rows_part, blocks, share, width), jnp.bfloat16),
        compiler_params=pltpu.CompilerParams(vmem_limit_bytes=48 * 2**20),
        cost_estimate=pl.CostEstimate(
            flops=2 * rows_part * blocks * channels * channels * width,
            bytes_accessed=4 * rows_part * blocks * channels * width,
            transcendentals=0,
        ),
        name="lift",
    )(scal, weight, columns)


def turn(angle_half):
    h = angle_half
    g = h * h
    s = 1.0
    for k in (6, 5, 4, 3, 2, 1):
        s = 1.0 - s * g * (1.0 / ((2 * k) * (2 * k + 1)))
    c = 1.0
    for k in (7, 6, 5, 4, 3, 2, 1):
        c = 1.0 - c * g * (1.0 / ((2 * k - 1) * (2 * k)))
    s = s * h
    return 1.0 - 2.0 * s * s, 2.0 * s * c


def fourier_kernel(scal_ref, wave_ref, x_ref, o_ref, keep_ref, *, row_at, groups):
    row = pl.program_id(1)
    rows_part = pl.num_programs(1)
    sources, _, blocks, share, width = x_ref.shape
    per = SPAN // width
    length = jnp.full((1, TILE), scal_ref[row_at + row], jnp.int32).astype(jnp.float32)
    inverse = 1.0 / length
    waves = wave_ref[...].astype(jnp.float32)

    at = lax.broadcasted_iota(jnp.int32, (FINE + COARSE + 16, TILE), 0)
    step = jnp.where(
        at < FINE, at, jnp.where(at < FINE + COARSE, (at - FINE) * FINE, (at - FINE - COARSE) * SPAN)
    ).astype(jnp.float32)
    product = step * waves
    residue = product - jnp.floor(product * inverse + 0.5) * length
    cosine, sine = turn(residue * inverse * math.pi)

    fine_cos, fine_sin = cosine[:FINE][None], sine[:FINE][None]
    coarse_cos = cosine[FINE : FINE + COARSE][:, None, :]
    coarse_sin = sine[FINE : FINE + COARSE][:, None, :]
    table_cos = (coarse_cos * fine_cos - coarse_sin * fine_sin).reshape(SPAN, TILE)
    table_sin = (coarse_sin * fine_cos + coarse_cos * fine_sin).reshape(SPAN, TILE)
    table = jnp.concatenate([table_cos.astype(jnp.bfloat16), table_sin.astype(jnp.bfloat16)], axis=1)

    x = x_ref[...].reshape(sources * blocks, share, width)[: groups * per]
    x = x.reshape(groups, per, share, width)
    if share % 16:
        x = x.astype(jnp.float32)
    x = jnp.concatenate([x[:, j].reshape(groups * share, width) for j in range(per)], axis=1)
    y = jnp.dot(x.astype(jnp.bfloat16), table, preferred_element_type=jnp.float32)
    y = y.reshape(groups, share, 2 * TILE)

    real = jnp.zeros((share, TILE), jnp.float32)
    imag = jnp.zeros((share, TILE), jnp.float32)
    for g in range(groups):
        k = FINE + COARSE + g
        c, s = cosine[k : k + 1], sine[k : k + 1]
        a, b = y[g, :, :TILE], y[g, :, TILE:]
        real = real + (c * a - s * b)
        imag = imag - (s * a + c * b)
    scale = lax.rsqrt(length)
    lanes = keep_ref.shape[1]
    fill = jnp.zeros((lanes - 2 * share, TILE), jnp.float32)
    both = jnp.concatenate([real * scale, imag * scale, fill], axis=0)
    rows_static = o_ref.shape[1]
    keep_ref[pl.ds(row, TILE, stride=rows_static), :] = both.T

    @pl.when(row == rows_part - 1)
    def _():
        o_ref[...] = keep_ref[...].reshape(o_ref.shape).astype(jnp.bfloat16)


def fourier(points, wave_order, scal, row_at):
    sources, rows_part, blocks, share, width = points.shape
    wave_count = wave_order.shape[0]
    total = sources * blocks * width
    groups = min(-(-LONGEST // SPAN), total // SPAN)
    lanes = -(-2 * share // 128) * 128
    return pl.pallas_call(
        functools.partial(fourier_kernel, row_at=row_at, groups=groups),
        grid_spec=pltpu.PrefetchScalarGridSpec(
            num_scalar_prefetch=1,
            grid=(wave_count // TILE, rows_part),
            in_specs=[
                pl.BlockSpec((1, TILE), lambda t, i, s: (0, t)),
                pl.BlockSpec((sources, 1, blocks, share, width), lambda t, i, s: (0, i, 0, 0, 0)),
            ],
            out_specs=pl.BlockSpec((TILE, rows_part, lanes), lambda t, i, s: (t, 0, 0)),
            scratch_shapes=[pltpu.VMEM((TILE * rows_part, lanes), jnp.float32)],
        ),
        out_shape=jax.ShapeDtypeStruct((wave_count, rows_part, lanes), jnp.bfloat16),
        compiler_params=pltpu.CompilerParams(vmem_limit_bytes=48 * 2**20),
        cost_estimate=pl.CostEstimate(
            flops=4 * rows_part * groups * SPAN * share * wave_count,
            bytes_accessed=2 * rows_part * wave_count * (lanes + total * share // TILE),
            transcendentals=0,
        ),
        name="fourier",
    )(scal, wave_order.reshape(1, wave_count), points)


def legendre_kernel(wave_ref, table_ref, *refs):
    pieces, o_ref = refs[:-1], refs[-1]
    slots, _, share, degrees = o_ref.shape
    _, rows, _ = table_ref.shape
    lanes = pieces[0].shape[-1]
    degree = lax.broadcasted_iota(jnp.int32, (2 * share, degrees), 1)
    for k in range(slots):
        parts = [p[:, k][:, None].astype(jnp.float32) for p in pieces]
        x = jnp.concatenate(parts, axis=1).reshape(rows, lanes)
        x = x.T[: 2 * share].astype(jnp.bfloat16)
        y = jnp.dot(x, table_ref[k], preferred_element_type=jnp.float32)
        y = jnp.where(degree >= wave_ref[pl.program_id(0) * slots + k], y, 0.0)
        o_ref[k, 0] = y[:share].astype(jnp.bfloat16)
        o_ref[k, 1] = y[share:].astype(jnp.bfloat16)


def legendre_sum(own_waves, legendre, pieces, share):
    slots_here, rows, degrees = legendre.shape
    sources, _, rows_part, lanes = pieces[0].shape
    piece_spec = pl.BlockSpec((sources, SLOTS, rows_part, lanes), lambda i, w: (0, i, 0, 0))
    return pl.pallas_call(
        legendre_kernel,
        grid_spec=pltpu.PrefetchScalarGridSpec(
            num_scalar_prefetch=1,
            grid=(slots_here // SLOTS,),
            in_specs=[pl.BlockSpec((SLOTS, rows, degrees), lambda i, w: (i, 0, 0))]
            + [piece_spec] * len(pieces),
            out_specs=pl.BlockSpec((SLOTS, 2, share, degrees), lambda i, w: (i, 0, 0, 0)),
        ),
        out_shape=jax.ShapeDtypeStruct((slots_here, 2, share, degrees), jnp.bfloat16),
        compiler_params=pltpu.CompilerParams(vmem_limit_bytes=48 * 2**20),
        cost_estimate=pl.CostEstimate(
            flops=4 * slots_here * rows * share * degrees,
            bytes_accessed=2 * slots_here * degrees * (rows + 2 * share),
            transcendentals=0,
        ),
        name="legendre",
    )(own_waves, legendre, *pieces)


def per_device(columns, vertical, row_len, wave_order, legendre):
    rows_here, blocks_here, channels, width = columns.shape
    levels = vertical.shape[0]
    wave_count = wave_order.shape[0]
    bands = lax.axis_size("band")
    levs = lax.axis_size("lev")
    slots_here = legendre.shape[0]
    share = channels // levs
    first = lax.axis_index("lev") * (blocks_here * width)
    scal = jnp.concatenate([row_len, first.reshape(1).astype(jnp.int32)])
    weight = jnp.kron(jnp.eye(channels // levels, dtype=vertical.dtype), vertical)
    own_waves = lax.dynamic_slice_in_dim(wave_order, lax.axis_index("band") * slots_here, slots_here)
    rows_part = rows_here // CHUNKS
    pieces = []
    for part in range(CHUNKS):
        lifted = lift(columns, weight, scal, part * rows_part, rows_part, levs)
        points = lax.all_to_all(lifted, "lev", split_axis=0, concat_axis=0, tiled=True)
        coeffs = fourier(points, wave_order, scal, part * rows_part)
        coeffs = coeffs.reshape(bands, slots_here, rows_part, coeffs.shape[-1])
        pieces.append(lax.all_to_all(coeffs, "band", split_axis=0, concat_axis=0, tiled=True))
    return legendre_sum(own_waves, legendre, pieces, share)


def solution(mesh):
    return jax.shard_map(
        per_device,
        mesh=mesh,
        in_specs=(P("band", "lev", None, None), P(), P("band"), P(), P("band", None, None)),
        out_specs=P("band", None, "lev", None),
        check_vma=False,
    )
```

```python
import functools
import math

import jax
import jax.numpy as jnp
from jax import lax
from jax.experimental import pallas as pl
from jax.experimental.pallas import tpu as pltpu
from jax.sharding import PartitionSpec as P

PARTS = (2, 1, 1)
LONGEST = 5136
FINE = 16
COARSE = 32
SPAN = FINE * COARSE
TILE = 640
SLOTS = 20


def lift_kernel(scal_ref, w_ref, x_ref, o_ref, *, row_at, rows):
    length = scal_ref[row_at + pl.program_id(0)]
    first = scal_ref[rows]
    targets, _, blocks, share, width = o_ref.shape
    for b in range(0, blocks, 2):
        pair = jnp.concatenate([x_ref[0, b], x_ref[0, b + 1]], axis=1)
        y = jnp.dot(w_ref[...], pair, preferred_element_type=jnp.float32)
        spot = first + b * width + lax.broadcasted_iota(jnp.int32, y.shape, 1)
        y = jnp.where(spot < length, y, 0.0)
        for h in range(2):
            part = y[:, h * width : (h + 1) * width].reshape(targets, share, width)
            o_ref[:, 0, b + h] = part.astype(jnp.bfloat16)


def lift(columns, weight, scal, row_at, rows_part, targets):
    rows, blocks, channels, width = columns.shape
    share = channels // targets
    return pl.pallas_call(
        functools.partial(lift_kernel, row_at=row_at, rows=rows),
        grid_spec=pltpu.PrefetchScalarGridSpec(
            num_scalar_prefetch=1,
            grid=(rows_part,),
            in_specs=[
                pl.BlockSpec((channels, channels), lambda i, s: (0, 0)),
                pl.BlockSpec((1, blocks, channels, width), lambda i, s: (row_at + i, 0, 0, 0)),
            ],
            out_specs=pl.BlockSpec((targets, 1, blocks, share, width), lambda i, s: (0, i, 0, 0, 0)),
        ),
        out_shape=jax.ShapeDtypeStruct((targets, rows_part, blocks, share, width), jnp.bfloat16),
        compiler_params=pltpu.CompilerParams(vmem_limit_bytes=48 * 2**20),
        cost_estimate=pl.CostEstimate(
            flops=2 * rows_part * blocks * channels * channels * width,
            bytes_accessed=4 * rows_part * blocks * channels * width,
            transcendentals=0,
        ),
        name="lift",
    )(scal, weight, columns)


def turn(angle_half):
    h = angle_half
    g = h * h
    s = 1.0
    for k in (6, 5, 4, 3, 2, 1):
        s = 1.0 - s * g * (1.0 / ((2 * k) * (2 * k + 1)))
    c = 1.0
    for k in (7, 6, 5, 4, 3, 2, 1):
        c = 1.0 - c * g * (1.0 / ((2 * k - 1) * (2 * k)))
    s = s * h
    return 1.0 - 2.0 * s * s, 2.0 * s * c


def fourier_kernel(scal_ref, wave_ref, x_ref, o_ref, keep_ref, *, row_at, groups):
    row = pl.program_id(1)
    rows_part = pl.num_programs(1)
    sources, _, blocks, share, width = x_ref.shape
    per = SPAN // width
    length = jnp.full((1, TILE), scal_ref[row_at + row], jnp.int32).astype(jnp.float32)
    inverse = 1.0 / length
    waves = wave_ref[...].astype(jnp.float32)

    at = lax.broadcasted_iota(jnp.int32, (FINE + COARSE + 16, TILE), 0)
    step = jnp.where(
        at < FINE, at, jnp.where(at < FINE + COARSE, (at - FINE) * FINE, (at - FINE - COARSE) * SPAN)
    ).astype(jnp.float32)
    product = step * waves
    residue = product - jnp.floor(product * inverse + 0.5) * length
    cosine, sine = turn(residue * inverse * math.pi)

    fine_cos, fine_sin = cosine[:FINE][None], sine[:FINE][None]
    coarse_cos = cosine[FINE : FINE + COARSE][:, None, :]
    coarse_sin = sine[FINE : FINE + COARSE][:, None, :]
    table_cos = (coarse_cos * fine_cos - coarse_sin * fine_sin).reshape(SPAN, TILE)
    table_sin = (coarse_sin * fine_cos + coarse_cos * fine_sin).reshape(SPAN, TILE)
    table = jnp.concatenate([table_cos.astype(jnp.bfloat16), table_sin.astype(jnp.bfloat16)], axis=1)

    x = x_ref[...].reshape(sources * blocks, share, width)[: groups * per]
    x = x.reshape(groups, per, share, width)
    if share % 16:
        x = x.astype(jnp.float32)
    x = jnp.concatenate([x[:, j].reshape(groups * share, width) for j in range(per)], axis=1)
    y = jnp.dot(x.astype(jnp.bfloat16), table, preferred_element_type=jnp.float32)
    y = y.reshape(groups, share, 2 * TILE)

    real = jnp.zeros((share, TILE), jnp.float32)
    imag = jnp.zeros((share, TILE), jnp.float32)
    for g in range(groups):
        k = FINE + COARSE + g
        c, s = cosine[k : k + 1], sine[k : k + 1]
        a, b = y[g, :, :TILE], y[g, :, TILE:]
        real = real + (c * a - s * b)
        imag = imag - (s * a + c * b)
    scale = lax.rsqrt(length)
    lanes = keep_ref.shape[1]
    fill = jnp.zeros((lanes - 2 * share, TILE), jnp.float32)
    both = jnp.concatenate([real * scale, imag * scale, fill], axis=0)
    rows_static = o_ref.shape[1]
    keep_ref[pl.ds(row, TILE, stride=rows_static), :] = both.T

    @pl.when(row == rows_part - 1)
    def _():
        o_ref[...] = keep_ref[...].reshape(o_ref.shape).astype(jnp.bfloat16)


def fourier(points, wave_order, scal, row_at):
    sources, rows_part, blocks, share, width = points.shape
    wave_count = wave_order.shape[0]
    total = sources * blocks * width
    groups = min(-(-LONGEST // SPAN), total // SPAN)
    lanes = -(-2 * share // 128) * 128
    return pl.pallas_call(
        functools.partial(fourier_kernel, row_at=row_at, groups=groups),
        grid_spec=pltpu.PrefetchScalarGridSpec(
            num_scalar_prefetch=1,
            grid=(wave_count // TILE, rows_part),
            in_specs=[
                pl.BlockSpec((1, TILE), lambda t, i, s: (0, t)),
                pl.BlockSpec((sources, 1, blocks, share, width), lambda t, i, s: (0, i, 0, 0, 0)),
            ],
            out_specs=pl.BlockSpec((TILE, rows_part, lanes), lambda t, i, s: (t, 0, 0)),
            scratch_shapes=[pltpu.VMEM((TILE * rows_part, lanes), jnp.float32)],
        ),
        out_shape=jax.ShapeDtypeStruct((wave_count, rows_part, lanes), jnp.bfloat16),
        compiler_params=pltpu.CompilerParams(vmem_limit_bytes=48 * 2**20),
        cost_estimate=pl.CostEstimate(
            flops=4 * rows_part * groups * SPAN * share * wave_count,
            bytes_accessed=2 * rows_part * (wave_count * lanes + total * share * (wave_count // TILE)),
            transcendentals=0,
        ),
        name="fourier",
    )(scal, wave_order.reshape(1, wave_count), points)


def legendre_kernel(wave_ref, table_ref, *refs):
    pieces, o_ref = refs[:-1], refs[-1]
    slots, _, share, degrees = o_ref.shape
    _, rows, _ = table_ref.shape
    lanes = pieces[0].shape[-1]
    degree = lax.broadcasted_iota(jnp.int32, (2 * share, degrees), 1)
    for k in range(slots):
        parts = [p[:, k].astype(jnp.float32) for p in pieces]
        x = jnp.concatenate(parts, axis=1).reshape(rows, lanes)
        x = x.T[: 2 * share].astype(jnp.bfloat16)
        y = jnp.dot(x, table_ref[k], preferred_element_type=jnp.float32)
        y = jnp.where(degree >= wave_ref[pl.program_id(0) * slots + k], y, 0.0)
        o_ref[k, 0] = y[:share].astype(jnp.bfloat16)
        o_ref[k, 1] = y[share:].astype(jnp.bfloat16)


def legendre_sum(own_waves, legendre, pieces, share):
    slots_here, rows, degrees = legendre.shape
    piece_specs = [
        pl.BlockSpec((p.shape[0], SLOTS, *p.shape[2:]), lambda i, w: (0, i, 0, 0)) for p in pieces
    ]
    return pl.pallas_call(
        legendre_kernel,
        grid_spec=pltpu.PrefetchScalarGridSpec(
            num_scalar_prefetch=1,
            grid=(slots_here // SLOTS,),
            in_specs=[pl.BlockSpec((SLOTS, rows, degrees), lambda i, w: (i, 0, 0))]
            + piece_specs,
            out_specs=pl.BlockSpec((SLOTS, 2, share, degrees), lambda i, w: (i, 0, 0, 0)),
        ),
        out_shape=jax.ShapeDtypeStruct((slots_here, 2, share, degrees), jnp.bfloat16),
        compiler_params=pltpu.CompilerParams(vmem_limit_bytes=48 * 2**20),
        cost_estimate=pl.CostEstimate(
            flops=4 * slots_here * rows * share * degrees,
            bytes_accessed=2 * slots_here * degrees * (rows + 2 * share),
            transcendentals=0,
        ),
        name="legendre",
    )(own_waves, legendre, *pieces)


def per_device(columns, vertical, row_len, wave_order, legendre):
    rows_here, blocks_here, channels, width = columns.shape
    levels = vertical.shape[0]
    wave_count = wave_order.shape[0]
    bands = lax.axis_size("band")
    levs = lax.axis_size("lev")
    slots_here = legendre.shape[0]
    share = channels // levs
    first = lax.axis_index("lev") * (blocks_here * width)
    scal = jnp.concatenate([row_len, first.reshape(1).astype(jnp.int32)])
    weight = jnp.kron(jnp.eye(channels // levels, dtype=vertical.dtype), vertical)
    own_waves = lax.dynamic_slice_in_dim(wave_order, lax.axis_index("band") * slots_here, slots_here)
    pieces = []
    row_at = 0
    for part in PARTS:
        rows_part = rows_here * part // sum(PARTS)
        lifted = lift(columns, weight, scal, row_at, rows_part, levs)
        points = lax.all_to_all(lifted, "lev", split_axis=0, concat_axis=0, tiled=True)
        coeffs = fourier(points, wave_order, scal, row_at)
        row_at += rows_part
        coeffs = coeffs.reshape(bands, slots_here, rows_part, coeffs.shape[-1])
        pieces.append(lax.all_to_all(coeffs, "band", split_axis=0, concat_axis=0, tiled=True))
    return legendre_sum(own_waves, legendre, pieces, share)


def solution(mesh):
    return jax.shard_map(
        per_device,
        mesh=mesh,
        in_specs=(P("band", "lev", None, None), P(), P("band"), P(), P("band", None, None)),
        out_specs=P("band", None, "lev", None),
        check_vma=False,
    )
```

```python
import functools
import math

import jax
import jax.numpy as jnp
from jax import lax
from jax.experimental import pallas as pl
from jax.experimental.pallas import tpu as pltpu
from jax.sharding import PartitionSpec as P

PARTS = (2, 1, 1)
LONGEST = 5136
FINE = 16
COARSE = 32
SPAN = FINE * COARSE
TILE = 640
SLOTS = 20


def lift_kernel(scal_ref, w_ref, x_ref, o_ref, *, row_at, rows):
    length = scal_ref[row_at + pl.program_id(0)]
    first = scal_ref[rows]
    targets, _, blocks, share, width = o_ref.shape
    for b in range(0, blocks, 2):
        pair = jnp.concatenate([x_ref[0, b], x_ref[0, b + 1]], axis=1)
        y = jnp.dot(w_ref[...], pair, preferred_element_type=jnp.float32)
        spot = first + b * width + lax.broadcasted_iota(jnp.int32, y.shape, 1)
        y = jnp.where(spot < length, y, 0.0)
        for h in range(2):
            part = y[:, h * width : (h + 1) * width].reshape(targets, share, width)
            o_ref[:, 0, b + h] = part.astype(jnp.bfloat16)


def lift(columns, weight, scal, row_at, rows_part, targets):
    rows, blocks, channels, width = columns.shape
    share = channels // targets
    return pl.pallas_call(
        functools.partial(lift_kernel, row_at=row_at, rows=rows),
        grid_spec=pltpu.PrefetchScalarGridSpec(
            num_scalar_prefetch=1,
            grid=(rows_part,),
            in_specs=[
                pl.BlockSpec((channels, channels), lambda i, s: (0, 0)),
                pl.BlockSpec((1, blocks, channels, width), lambda i, s: (row_at + i, 0, 0, 0)),
            ],
            out_specs=pl.BlockSpec((targets, 1, blocks, share, width), lambda i, s: (0, i, 0, 0, 0)),
        ),
        out_shape=jax.ShapeDtypeStruct((targets, rows_part, blocks, share, width), jnp.bfloat16),
        compiler_params=pltpu.CompilerParams(vmem_limit_bytes=48 * 2**20),
        cost_estimate=pl.CostEstimate(
            flops=2 * rows_part * blocks * channels * channels * width,
            bytes_accessed=4 * rows_part * blocks * channels * width,
            transcendentals=0,
        ),
        name="lift",
    )(scal, weight, columns)


def turn(angle_half):
    h = angle_half
    g = h * h
    s = 1.0
    for k in (6, 5, 4, 3, 2, 1):
        s = 1.0 - s * g * (1.0 / ((2 * k) * (2 * k + 1)))
    c = 1.0
    for k in (7, 6, 5, 4, 3, 2, 1):
        c = 1.0 - c * g * (1.0 / ((2 * k - 1) * (2 * k)))
    s = s * h
    return 1.0 - 2.0 * s * s, 2.0 * s * c


def fourier_kernel(scal_ref, wave_ref, x_ref, o_ref, keep_ref, *, row_at, groups):
    row = pl.program_id(1)
    rows_part = pl.num_programs(1)
    sources, _, blocks, share, width = x_ref.shape
    per = SPAN // width
    length = jnp.full((1, TILE), scal_ref[row_at + row], jnp.int32).astype(jnp.float32)
    inverse = 1.0 / length
    waves = wave_ref[...].astype(jnp.float32)

    at = lax.broadcasted_iota(jnp.int32, (FINE + COARSE + 16, TILE), 0)
    step = jnp.where(
        at < FINE, at, jnp.where(at < FINE + COARSE, (at - FINE) * FINE, (at - FINE - COARSE) * SPAN)
    ).astype(jnp.float32)
    product = step * waves
    residue = product - jnp.floor(product * inverse + 0.5) * length
    cosine, sine = turn(residue * inverse * math.pi)

    fine_cos, fine_sin = cosine[:FINE][None], sine[:FINE][None]
    coarse_cos = cosine[FINE : FINE + COARSE][:, None, :]
    coarse_sin = sine[FINE : FINE + COARSE][:, None, :]
    table_cos = (coarse_cos * fine_cos - coarse_sin * fine_sin).reshape(SPAN, TILE)
    table_sin = (coarse_sin * fine_cos + coarse_cos * fine_sin).reshape(SPAN, TILE)
    table = jnp.concatenate([table_cos.astype(jnp.bfloat16), table_sin.astype(jnp.bfloat16)], axis=1)

    x = x_ref[...].reshape(sources * blocks, share, width)[: groups * per]
    x = x.reshape(groups, per, share, width)
    if share % 16:
        x = x.astype(jnp.float32)
    x = jnp.concatenate([x[:, j].reshape(groups * share, width) for j in range(per)], axis=1)
    y = jnp.dot(x.astype(jnp.bfloat16), table, preferred_element_type=jnp.float32)
    y = y.reshape(groups, share, 2 * TILE)

    real = jnp.zeros((share, TILE), jnp.float32)
    imag = jnp.zeros((share, TILE), jnp.float32)
    for g in range(groups):
        k = FINE + COARSE + g
        c, s = cosine[k : k + 1], sine[k : k + 1]
        a, b = y[g, :, :TILE], y[g, :, TILE:]
        real = real + (c * a - s * b)
        imag = imag - (s * a + c * b)
    scale = lax.rsqrt(length)
    lanes = keep_ref.shape[1]
    fill = jnp.zeros((lanes - 2 * share, TILE), jnp.float32)
    both = jnp.concatenate([real * scale, imag * scale, fill], axis=0)
    rows_static = o_ref.shape[1]
    keep_ref[pl.ds(row, TILE, stride=rows_static), :] = both.T

    @pl.when(row == rows_part - 1)
    def _():
        o_ref[...] = keep_ref[...].reshape(o_ref.shape).astype(jnp.bfloat16)


def fourier(points, wave_order, scal, row_at):
    sources, rows_part, blocks, share, width = points.shape
    wave_count = wave_order.shape[0]
    total = sources * blocks * width
    groups = min(-(-LONGEST // SPAN), total // SPAN)
    lanes = -(-2 * share // 128) * 128
    return pl.pallas_call(
        functools.partial(fourier_kernel, row_at=row_at, groups=groups),
        grid_spec=pltpu.PrefetchScalarGridSpec(
            num_scalar_prefetch=1,
            grid=(wave_count // TILE, rows_part),
            in_specs=[
                pl.BlockSpec((1, TILE), lambda t, i, s: (0, t)),
                pl.BlockSpec((sources, 1, blocks, share, width), lambda t, i, s: (0, i, 0, 0, 0)),
            ],
            out_specs=pl.BlockSpec((TILE, rows_part, lanes), lambda t, i, s: (t, 0, 0)),
            scratch_shapes=[pltpu.VMEM((TILE * rows_part, lanes), jnp.float32)],
        ),
        out_shape=jax.ShapeDtypeStruct((wave_count, rows_part, lanes), jnp.bfloat16),
        compiler_params=pltpu.CompilerParams(vmem_limit_bytes=48 * 2**20),
        cost_estimate=pl.CostEstimate(
            flops=4 * rows_part * groups * SPAN * share * wave_count,
            bytes_accessed=2 * rows_part * (wave_count * lanes + total * share * (wave_count // TILE)),
            transcendentals=0,
        ),
        name="fourier",
    )(scal, wave_order.reshape(1, wave_count), points)


def legendre_kernel(wave_ref, table_ref, *refs):
    pieces, o_ref = refs[:-1], refs[-1]
    slots, _, share, degrees = o_ref.shape
    _, rows, _ = table_ref.shape
    lanes = pieces[0].shape[-1]
    degree = lax.broadcasted_iota(jnp.int32, (2 * share, degrees), 1)
    for k in range(slots):
        parts = [p[:, k].astype(jnp.float32) for p in pieces]
        x = jnp.concatenate(parts, axis=1).reshape(rows, lanes)
        x = x.T[: 2 * share].astype(jnp.bfloat16)
        y = jnp.dot(x, table_ref[k], preferred_element_type=jnp.float32)
        y = jnp.where(degree >= wave_ref[pl.program_id(0) * slots + k], y, 0.0)
        o_ref[k, 0] = y[:share].astype(jnp.bfloat16)
        o_ref[k, 1] = y[share:].astype(jnp.bfloat16)


def legendre_sum(own_waves, legendre, pieces, share):
    slots_here, rows, degrees = legendre.shape
    piece_specs = [
        pl.BlockSpec((p.shape[0], SLOTS, *p.shape[2:]), lambda i, w: (0, i, 0, 0)) for p in pieces
    ]
    return pl.pallas_call(
        legendre_kernel,
        grid_spec=pltpu.PrefetchScalarGridSpec(
            num_scalar_prefetch=1,
            grid=(slots_here // SLOTS,),
            in_specs=[pl.BlockSpec((SLOTS, rows, degrees), lambda i, w: (i, 0, 0))]
            + piece_specs,
            out_specs=pl.BlockSpec((SLOTS, 2, share, degrees), lambda i, w: (i, 0, 0, 0)),
        ),
        out_shape=jax.ShapeDtypeStruct((slots_here, 2, share, degrees), jnp.bfloat16),
        compiler_params=pltpu.CompilerParams(vmem_limit_bytes=48 * 2**20),
        cost_estimate=pl.CostEstimate(
            flops=4 * slots_here * rows * share * degrees,
            bytes_accessed=2 * slots_here * degrees * (rows + 2 * share),
            transcendentals=0,
        ),
        name="legendre",
    )(own_waves, legendre, *pieces)


def exchange(blocks, axis):
    count, me = blocks.shape[0], lax.axis_index(axis)
    out, early = blocks, None
    for d in range(1, count):
        block = lax.dynamic_index_in_dim(blocks, lax.rem(me + d, count), 0)
        block = lax.ppermute(block, axis, [(i, (i + d) % count) for i in range(count)])
        early = block if d == 1 else early
        out = lax.dynamic_update_index_in_dim(out, block, lax.rem(me + count - d, count), 0)
    return out, early


def per_device(columns, vertical, row_len, wave_order, legendre):
    rows_here, blocks_here, channels, width = columns.shape
    levels = vertical.shape[0]
    wave_count = wave_order.shape[0]
    bands = lax.axis_size("band")
    levs = lax.axis_size("lev")
    slots_here = legendre.shape[0]
    share = channels // levs
    first = lax.axis_index("lev") * (blocks_here * width)
    scal = jnp.concatenate([row_len, first.reshape(1).astype(jnp.int32)])
    weight = jnp.kron(jnp.eye(channels // levels, dtype=vertical.dtype), vertical)
    own_waves = lax.dynamic_slice_in_dim(wave_order, lax.axis_index("band") * slots_here, slots_here)
    pieces, received, points, points_at = [], [], None, 0
    row_at = 0
    for part in PARTS:
        rows_part = rows_here * part // sum(PARTS)
        lifted = lift(columns, weight, scal, row_at, rows_part, levs)
        if points is not None:
            lifted, points = lax.optimization_barrier((lifted, points))
        following, early = exchange(lifted, "lev")
        if points is not None:
            points, _ = lax.optimization_barrier((points, early))
            received.append((points, points_at))
        points, points_at = following, row_at
        row_at += rows_part
    received.append((points, points_at))
    for points, row_at in received:
        coeffs = fourier(points, wave_order, scal, row_at)
        coeffs = coeffs.reshape(bands, slots_here, *coeffs.shape[1:])
        pieces.append(lax.all_to_all(coeffs, "band", split_axis=0, concat_axis=0, tiled=True))
    return legendre_sum(own_waves, legendre, pieces, share)


def solution(mesh):
    return jax.shard_map(
        per_device,
        mesh=mesh,
        in_specs=(P("band", "lev", None, None), P(), P("band"), P(), P("band", None, None)),
        out_specs=P("band", None, "lev", None),
        check_vma=False,
    )
```
